32 devices in a mesh: row: 8 (over z, y), col: 4 (over x, core).
Axes of the slice: x: 2, y: 2, z: 4, core: 2. Of those that a mesh axis runs over, the one named last changes fastest.
Arguments:
- a_slab: float32 [4096, 1024], P('row', 'col'), may hold values from -6 to 6
- b_panel: float32 [1024, 16384], P('row', 'col'), may hold values from -0.1875 to 0.1875
- row_weights: float32 [2, 4096], P(None, 'row'), may hold values from -0.09375 to 0.09375
- col_weights: float32 [2, 16384], P(None, 'col'), may hold values from -0.046875 to 0.046875
Outputs:
- product: float32 [4096, 16384], P('row', 'col')
- check_rows: float32 [2, 16384], P(None, 'col')
- check_cols: float32 [2, 4096], P(None, 'row')
The draws below stay inside these ranges and needn't reach their ends.
All inputs are finite; a program needn't handle non-finite values.
Results may differ from the reference program's by a relative error of at most 0.000076.
Values sent between devices are 32-bit elements; how exact they have to be, the bound alone decides.
A program may use at most 64 MiB of HBM per device.

```python
import jax
import jax.numpy as jnp
from jax import lax

M = 4096
N = 16384
K = 1024


def steps_of(key, extent, pieces, least, largest):
    def one(axis_at, shards_of):
        steps = jax.random.uniform(jax.random.fold_in(jax.random.fold_in(key, 6), axis_at), (shards_of,), jnp.float32, least / len(pieces), largest / len(pieces))
        return jnp.repeat(jnp.exp(steps), extent[axis_at] // shards_of).reshape((-1,) + (1,) * (len(extent) - axis_at - 1))

    level = one(*pieces[0])
    for cut in pieces[1:]:
        level = level * one(*cut)
    return level


def noise(rng, shape, deviation, bound, pieces=(), dtype=jnp.bfloat16):
    entries = deviation * jax.random.normal(rng, shape, jnp.float32)
    if pieces:
        entries = entries * steps_of(rng, shape, pieces, -0.22, 0.18)
    return jnp.clip(entries, -bound, bound).astype(dtype)


def setup_inputs(seed: int = 0) -> dict:
    key_list = jax.random.split(jax.random.key(seed), 5)
    return {
        "a_slab": noise(key_list[0], (M, K), 1.0, 6.0, ((0, 8), (1, 4)), jnp.float32),
        "b_panel": noise(key_list[1], (K, N), K ** -0.5, 0.1875, ((0, 8), (1, 4)), jnp.float32),
        "row_weights": noise(key_list[2], (2, M), M ** -0.5, 0.09375, ((1, 8),), jnp.float32),
        "col_weights": noise(key_list[3], (2, N), N ** -0.5, 0.046875, ((1, 4),), jnp.float32),
    }


def matmul(left, right):
    return jnp.dot(left, right, precision=lax.Precision.HIGHEST, preferred_element_type=jnp.float32)


def reference(a_slab, b_panel, row_weights, col_weights):
    product = matmul(a_slab, b_panel)
    a_check = matmul(row_weights, a_slab)
    b_check = matmul(b_panel, col_weights.T)
    check_rows = matmul(a_check, b_panel)
    check_cols = matmul(a_slab, b_check).T
    return product, check_rows, check_cols
```

```python
import jax
import jax.numpy as jnp
from jax import lax
from jax.sharding import PartitionSpec as P


def dot(left, right, dims):
    return lax.dot_general(
        left, right, (dims, ((), ())), precision=lax.Precision.HIGH, preferred_element_type=jnp.float32
    )


def per_device(a_slab, b_panel, row_weights, col_weights):
    b_whole = lax.all_gather(b_panel, "row", axis=0, tiled=True)
    a_whole = lax.all_gather(a_slab, "col", axis=1, tiled=True)
    a_part = lax.psum(dot(row_weights, a_slab, ((1,), (0,))), "row")
    a_check = lax.all_gather(a_part, "col", axis=1, tiled=True)
    b_part = lax.psum(dot(col_weights, b_panel, ((1,), (1,))), "col")
    b_check = lax.all_gather(b_part, "row", axis=1, tiled=True)
    check_cols = dot(b_check, a_whole, ((1,), (1,)))
    product = dot(a_whole, b_whole, ((1,), (0,)))
    check_rows = dot(a_check, b_whole, ((1,), (0,)))
    return (product, check_rows, check_cols)


def solution(mesh):
    placed = (P("row", "col"), P("row", "col"), P(None, "row"), P(None, "col"))
    return jax.shard_map(
        per_device,
        mesh=mesh,
        in_specs=placed,
        out_specs=(P("row", "col"), P(None, "col"), P(None, "row")),
        check_vma=False,
    )
```

```python
import functools

import jax
import jax.numpy as jnp
from jax import lax
from jax.experimental import pallas as pl
from jax.experimental.pallas import tpu as pltpu
from jax.sharding import PartitionSpec as P

MESH = pl.DeviceIdType.MESH
WIDTH = 256
AHEAD = 3


def exact_dot(left, right, dims):
    return lax.dot_general(
        left, right, (dims, ((), ())), precision=lax.Precision.HIGHEST, preferred_element_type=jnp.float32
    )


def split(value):
    high = value.astype(jnp.bfloat16)
    return high, (value - high.astype(jnp.float32)).astype(jnp.bfloat16)


def kernel(
    R, C, a_ref, b_ref, rw_ref, cw_ref, prod, rows_out, cols_out,
    bbuf, obuf, abuf, a_hi, a_lo, chk, rwp, cwp, sa, sb, ga, gb, bchk,
    local_sem, y_send, y_recv, up_send, dn_send, z_recv, a_send, a_recv,
    sa_send, sa_recv, sb_send, sb_recv, ga_send, ga_recv, gb_send, gb_recv,
    o_local, o_send, o_recv, c_send, c_recv,
):
    Z, G = R // 2, C // 2
    r, c = lax.axis_index("row"), lax.axis_index("col")
    z, y = r // 2, lax.rem(r, 2)
    mate = r + 1 - 2 * y
    sib = c + 1 - 2 * lax.rem(c, 2)
    m, kc = a_ref.shape
    kb, n = b_ref.shape
    H = n // 2
    W = WIDTH
    NC = H // W

    def remote(src, dst, ssem, rsem, where):
        return pltpu.make_async_remote_copy(
            src_ref=src, dst_ref=dst, send_sem=ssem, recv_sem=rsem, device_id=where, device_id_type=MESH
        )

    def same(ref, ssem, rsem, where):
        return remote(ref, ref, ssem, rsem, where)

    barrier = pltpu.get_barrier_semaphore()
    row_peers = [lax.rem(r + d, R) for d in range(1, R)]
    col_peers = [lax.rem(c + d, C) for d in range(1, C)]
    for p in row_peers:
        pl.semaphore_signal(barrier, inc=1, device_id={"row": p}, device_id_type=MESH)
    for p in col_peers:
        pl.semaphore_signal(barrier, inc=1, device_id={"col": p}, device_id_type=MESH)
    own = pltpu.make_async_copy(b_ref.at[:, pl.ds(pl.multiple_of(y * H, H), H)], bbuf.at[r], local_sem)
    own.start()
    abuf[0, c] = a_ref[...]
    pl.semaphore_wait(barrier, R - 1 + C - 1)

    def columns(j):
        return pl.ds(pl.multiple_of(j * W, W), W)

    def y_copy(j):
        src = b_ref.at[:, pl.ds(pl.multiple_of((1 - y) * H + j * W, W), W)]
        return remote(src, bbuf.at[r, :, columns(j)], y_send.at[j], y_recv.at[j], {"row": mate})

    def unit(u, j, to, ssem):
        return same(bbuf.at[pl.ds(2 * u, 2), :, columns(j)], ssem.at[u, j], z_recv.at[u, j], {"row": to})

    def up(u, j):
        return unit(u, j, r + 2, up_send)

    def down(u, j):
        return unit(u, j, r - 2, dn_send)

    same_core = [lax.rem(c + 2 * k, C) for k in range(1, G)]
    a_sends = []

    def a_copy(s, cc, t, where):
        copy = remote(abuf.at[s, cc], abuf.at[t, cc], a_send.at[len(a_sends)], a_recv.at[t, cc], where)
        a_sends.append(copy)
        copy.start()

    def a_wait(t, cc):
        remote(abuf.at[t, cc], abuf.at[t, cc], a_send.at[0], a_recv.at[t, cc], {"row": mate}).wait_recv()

    y_copy(0).start()
    a_copy(0, c, 1, {"row": mate})
    for p in same_core:
        a_copy(0, c, 0, {"col": p})
    a_copy(0, c, 0, {"col": sib})

    @pl.loop(1, NC)
    def _(j):
        y_copy(j).start()

    own.wait()

    def send_own(j):
        y_copy(j).wait_recv()

        @pl.when(z < Z - 1)
        def _():
            up(z, j).start()

        @pl.when(z > 0)
        def _():
            down(z, j).start()

    for j in range(AHEAD):
        send_own(j)

    def forward(j):
        @pl.when(j + AHEAD < NC)
        def _():
            send_own(j + AHEAD)

        for d in range(1, Z):
            @pl.when(z - d >= 0)
            def _():
                up(z - d, j).wait_recv()

                @pl.when(z < Z - 1)
                def _():
                    up(z - d, j).start()

            @pl.when(z + d < Z)
            def _():
                down(z + d, j).wait_recv()

                @pl.when(z > 0)
                def _():
                    down(z + d, j).start()

    rwp[...] = jnp.zeros_like(rwp)
    cwp[...] = jnp.zeros_like(cwp)
    rwp[0:2, :] = rw_ref[...]
    cwp[0:2, :] = cw_ref[...]
    sa[r] = exact_dot(rwp[...], a_ref[...], ((1,), (0,)))
    sb[c] = exact_dot(cwp[...], b_ref[...], ((1,), (1,)))

    def spread(buf, slot, peers, axis, ssem, rsem):
        copies = [
            same(buf.at[slot], ssem.at[i], rsem.at[slot], {axis: p}) for i, p in enumerate(peers)
        ]
        for copy in copies:
            copy.start()
        return copies

    def collect(buf, peers, axis, ssem, rsem):
        for p in peers:
            same(buf.at[p], ssem.at[0], rsem.at[p], {axis: p}).wait_recv()

    small = spread(sa, r, row_peers, "row", sa_send, sa_recv)
    small += spread(sb, c, col_peers, "col", sb_send, sb_recv)

    a_wait(1, c)
    for p in same_core:
        a_copy(1, c, 1, {"col": p})
    a_copy(1, c, 1, {"col": sib})

    collect(sa, row_peers, "row", sa_send, sa_recv)
    collect(sb, col_peers, "col", sb_send, sb_recv)
    ga[c] = jnp.sum(sa[...], axis=0)
    gb[r] = jnp.sum(sb[...], axis=0)
    small += spread(ga, c, col_peers, "col", ga_send, ga_recv)
    small += spread(gb, r, row_peers, "row", gb_send, gb_recv)

    forward(0)

    for t in range(2):
        for p in same_core:
            a_wait(t, p)
            a_copy(t, p, t, {"col": sib})
    collect(ga, col_peers, "col", ga_send, ga_recv)
    collect(gb, row_peers, "row", gb_send, gb_recv)

    forward(1)

    for t in range(2):
        for k in range(G):
            a_wait(t, lax.rem(sib + 2 * k, C))
    for i in range(R):
        bchk[:, i * kb:(i + 1) * kb] = gb[i]
    for i in range(C):
        span = slice(i * kc, (i + 1) * kc)
        for t in range(2):
            high, low = split(abuf[t, i])
            a_hi[t * m:(t + 1) * m, span] = high
            a_lo[t * m:(t + 1) * m, span] = low
        high, low = split(jnp.concatenate([ga[i], jnp.zeros_like(ga[i])], axis=0))
        a_hi[2 * m:2 * m + 16, span] = high
        a_lo[2 * m:2 * m + 16, span] = low
    total = jnp.zeros((8, m), jnp.float32)
    for i in range(C):
        total += exact_dot(bchk[:, i * kc:(i + 1) * kc], abuf[0, i], ((1,), (1,)))
    cols_out[...] = total[0:2]

    def out_local(j):
        return pltpu.make_async_copy(
            obuf.at[j, 0:m], prod.at[:, pl.ds(pl.multiple_of(y * H + j * W, W), W)], o_local.at[j]
        )

    def out_remote(j):
        dst = prod.at[:, pl.ds(pl.multiple_of(y * H + j * W, W), W)]
        return remote(obuf.at[j, m:2 * m], dst, o_send.at[j], o_recv.at[j], {"row": mate})

    def dot(left, right):
        return jnp.dot(left, right, preferred_element_type=jnp.float32)

    @pl.loop(0, NC)
    def _(j):
        @pl.when(j >= 2)
        def _():
            forward(j)

        high, low = split(bbuf[:, :, columns(j)].reshape(R * kb, W))
        acc = dot(a_hi[...], high) + dot(a_hi[...], low) + dot(a_lo[...], high)
        obuf[j] = acc[0:2 * m]
        chk[y, :, columns(j)] = acc[2 * m:2 * m + 8]
        out_remote(j).start()
        out_local(j).start()

    last = same(chk.at[y], c_send, c_recv, {"row": mate})
    last.start()

    @pl.loop(0, NC)
    def _(j):
        y_copy(j).wait_send()
        for u in range(Z):
            @pl.when((z < Z - 1) & (u <= z))
            def _():
                up(u, j).wait_send()

            @pl.when((z > 0) & (u >= z))
            def _():
                down(u, j).wait_send()

    for copy in a_sends + small:
        copy.wait_send()
    last.wait()
    rows_out[:, 0:H] = chk[0, 0:2, :]
    rows_out[:, H:2 * H] = chk[1, 0:2, :]

    @pl.loop(0, NC)
    def _(j):
        out_local(j).wait()
        out_remote(j).wait()


def per_device(R, C, a_slab, b_panel, row_weights, col_weights):
    m, kc = a_slab.shape
    kb, n = b_panel.shape
    Z, G, H = R // 2, C // 2, n // 2
    NC = H // WIDTH
    K = R * kb
    f32, bf16 = jnp.float32, jnp.bfloat16
    dma = pltpu.SemaphoreType.DMA
    vmem = pl.BlockSpec(memory_space=pltpu.VMEM)
    scratch = [
        pltpu.VMEM((R, kb, H), f32),
        pltpu.VMEM((NC, 2 * m, WIDTH), f32),
        pltpu.VMEM((2, C, m, kc), f32),
        pltpu.VMEM((2 * m + 16, K), bf16),
        pltpu.VMEM((2 * m + 16, K), bf16),
        pltpu.VMEM((2, 8, H), f32),
        pltpu.VMEM((8, m), f32),
        pltpu.VMEM((8, n), f32),
        pltpu.VMEM((R, 8, kc), f32),
        pltpu.VMEM((C, 8, kb), f32),
        pltpu.VMEM((C, 8, kc), f32),
        pltpu.VMEM((R, 8, kb), f32),
        pltpu.VMEM((8, K), f32),
        dma,
        dma((NC,)), dma((NC,)),
        dma((Z, NC)), dma((Z, NC)), dma((Z, NC)),
        dma((3 + 4 * (G - 1),)), dma((2, C)),
        dma((R,)), dma((R,)), dma((C,)), dma((C,)),
        dma((C,)), dma((C,)), dma((R,)), dma((R,)),
        dma((NC,)), dma((NC,)), dma((NC,)),
        dma, dma,
    ]
    return pl.pallas_call(
        functools.partial(kernel, R, C),
        out_shape=(
            jax.ShapeDtypeStruct((m, n), f32),
            jax.ShapeDtypeStruct((2, n), f32),
            jax.ShapeDtypeStruct((2, m), f32),
        ),
        in_specs=[vmem] * 4,
        out_specs=(pl.BlockSpec(memory_space=pl.ANY), vmem, vmem),
        scratch_shapes=scratch,
        compiler_params=pltpu.CompilerParams(
            collective_id=0, has_side_effects=True, vmem_limit_bytes=56 * 1024 * 1024
        ),
    )(a_slab, b_panel, row_weights, col_weights)


def solution(mesh):
    placed = (P("row", "col"), P("row", "col"), P(None, "row"), P(None, "col"))
    return jax.shard_map(
        functools.partial(per_device, mesh.shape["row"], mesh.shape["col"]),
        mesh=mesh,
        in_specs=placed,
        out_specs=(P("row", "col"), P(None, "col"), P(None, "row")),
        check_vma=False,
    )
```

```python
import functools

import jax
import jax.numpy as jnp
from jax import lax
from jax.experimental import pallas as pl
from jax.experimental.pallas import tpu as pltpu
from jax.sharding import PartitionSpec as P

MESH = pl.DeviceIdType.MESH
WIDTH = 128
AHEAD = 6
PACE = 6


def exact_dot(left, right, dims):
    return lax.dot_general(
        left, right, (dims, ((), ())), precision=lax.Precision.HIGHEST, preferred_element_type=jnp.float32
    )


def split(value):
    high = value.astype(jnp.bfloat16)
    return high, (value - high.astype(jnp.float32)).astype(jnp.bfloat16)


def kernel(
    R, C, a_ref, b_ref, rw_ref, cw_ref, prod, rows_out, cols_out,
    bbuf, obuf, abuf, a_hi, a_lo, chk, rwp, cwp, sa, sb, ga, gb, bchk,
    local_sem, y_send, y_recv, up_send, dn_send, z_recv, a_send, a_recv,
    sa_send, sa_recv, sb_send, sb_recv, ga_send, ga_recv, gb_send, gb_recv,
    o_send, o_recv, c_send, c_recv,
):
    Z, G = R // 2, C // 2
    r, c = lax.axis_index("row"), lax.axis_index("col")
    z, y = r // 2, lax.rem(r, 2)
    mate = r + 1 - 2 * y
    sib = c + 1 - 2 * lax.rem(c, 2)
    m, kc = a_ref.shape
    kb, n = b_ref.shape
    H = n // 2
    W = WIDTH
    NC = H // W

    def remote(src, dst, ssem, rsem, where):
        return pltpu.make_async_remote_copy(
            src_ref=src, dst_ref=dst, send_sem=ssem, recv_sem=rsem, device_id=where, device_id_type=MESH
        )

    def same(ref, ssem, rsem, where):
        return remote(ref, ref, ssem, rsem, where)

    barrier = pltpu.get_barrier_semaphore()
    row_peers = [lax.rem(r + d, R) for d in range(1, R)]
    col_peers = [lax.rem(c + d, C) for d in range(1, C)]
    for p in row_peers:
        pl.semaphore_signal(barrier, inc=1, device_id={"row": p}, device_id_type=MESH)
    for p in col_peers:
        pl.semaphore_signal(barrier, inc=1, device_id={"col": p}, device_id_type=MESH)
    own = pltpu.make_async_copy(b_ref.at[:, pl.ds(pl.multiple_of(y * H, H), H)], bbuf.at[r], local_sem)
    own.start()
    abuf[0, c] = a_ref[...]
    pl.semaphore_wait(barrier, R - 1 + C - 1)

    def columns(j):
        return pl.ds(pl.multiple_of(j * W, W), W)

    def y_copy(j):
        src = b_ref.at[:, pl.ds(pl.multiple_of((1 - y) * H + j * W, W), W)]
        return remote(src, bbuf.at[r, :, columns(j)], y_send.at[j], y_recv.at[j], {"row": mate})

    def unit(u, j, to, ssem):
        return same(bbuf.at[pl.ds(2 * u, 2), :, columns(j)], ssem.at[2 * u, j], z_recv.at[u, j], {"row": to})

    def up(u, j):
        return unit(u, j, r + 2, up_send)

    def down(u, j):
        return unit(u, j, r - 2, dn_send)

    same_core = [lax.rem(c + 2 * k, C) for k in range(1, G)]
    a_sends = []

    def a_copy(s, cc, t, where):
        copy = remote(abuf.at[s, cc], abuf.at[t, cc], a_send.at[len(a_sends)], a_recv.at[t, cc], where)
        a_sends.append(copy)
        copy.start()

    def a_wait(t, cc):
        remote(abuf.at[t, cc], abuf.at[t, cc], a_send.at[0], a_recv.at[t, cc], {"row": mate}).wait_recv()

    a_copy(0, c, 1, {"row": mate})
    for p in same_core:
        a_copy(0, c, 0, {"col": p})
    a_copy(0, c, 0, {"col": sib})
    for j in range(2):
        y_copy(j).start()

    def own_block(row, j, to, ssem):
        src = dst = bbuf.at[row, :, columns(j)]
        if row is r:
            src = b_ref.at[:, pl.ds(pl.multiple_of(y * H + j * W, W), W)]
        return remote(src, dst, ssem.at[row, j], z_recv.at[z, j], {"row": to})

    def send_block(row, j):
        @pl.when(z < Z - 1)
        def _():
            own_block(row, j, r + 2, up_send).start()

        @pl.when(z > 0)
        def _():
            own_block(row, j, r - 2, dn_send).start()

    @pl.loop(0, NC)
    def _(j):
        send_block(r, j)

    def send_mate(j):
        y_copy(j).wait_recv()
        send_block(mate, j)

        @pl.when(j + PACE < NC)
        def _():
            y_copy(j + PACE).start()

    def forward(j):
        @pl.when(j + AHEAD < NC)
        def _():
            send_mate(j + AHEAD)

        for d in range(1, Z):
            @pl.when(z - d >= 0)
            def _():
                up(z - d, j).wait_recv()

                @pl.when(z < Z - 1)
                def _():
                    up(z - d, j).start()

            @pl.when(z + d < Z)
            def _():
                down(z + d, j).wait_recv()

                @pl.when(z > 0)
                def _():
                    down(z + d, j).start()

    rwp[...] = jnp.zeros_like(rwp)
    cwp[...] = jnp.zeros_like(cwp)
    rwp[0:2, :] = rw_ref[...]
    cwp[0:2, :] = cw_ref[...]
    sa[r] = exact_dot(rwp[...], a_ref[...], ((1,), (0,)))
    sb[c] = exact_dot(cwp[...], b_ref[...], ((1,), (1,)))

    def spread(buf, slot, peers, axis, ssem, rsem):
        copies = [
            same(buf.at[slot], ssem.at[i], rsem.at[slot], {axis: p}) for i, p in enumerate(peers)
        ]
        for copy in copies:
            copy.start()
        return copies

    def collect(buf, peers, axis, ssem, rsem):
        for p in peers:
            same(buf.at[p], ssem.at[0], rsem.at[p], {axis: p}).wait_recv()

    small = spread(sa, r, row_peers, "row", sa_send, sa_recv)
    small += spread(sb, c, col_peers, "col", sb_send, sb_recv)

    a_wait(1, c)
    for p in same_core:
        a_copy(1, c, 1, {"col": p})
    a_copy(1, c, 1, {"col": sib})
    for j in range(2, PACE):
        y_copy(j).start()
    for j in range(3):
        send_mate(j)

    collect(sa, row_peers, "row", sa_send, sa_recv)
    collect(sb, col_peers, "col", sb_send, sb_recv)
    ga[c] = jnp.sum(sa[...], axis=0)
    gb[r] = jnp.sum(sb[...], axis=0)
    small += spread(ga, c, col_peers, "col", ga_send, ga_recv)
    small += spread(gb, r, row_peers, "row", gb_send, gb_recv)

    for j in range(3, AHEAD):
        send_mate(j)

    for t in range(2):
        for p in same_core:
            a_wait(t, p)
            a_copy(t, p, t, {"col": sib})
    collect(ga, col_peers, "col", ga_send, ga_recv)
    collect(gb, row_peers, "row", gb_send, gb_recv)

    forward(0)

    for t in range(2):
        for k in range(G):
            a_wait(t, lax.rem(sib + 2 * k, C))
    for i in range(R):
        bchk[:, i * kb:(i + 1) * kb] = gb[i]
    for i in range(C):
        span = slice(i * kc, (i + 1) * kc)
        for t in range(2):
            high, low = split(abuf[t, i])
            a_hi[t * m:(t + 1) * m, span] = high
            a_lo[t * m:(t + 1) * m, span] = low
        high, low = split(jnp.concatenate([ga[i], jnp.zeros_like(ga[i])], axis=0))
        a_hi[2 * m:2 * m + 16, span] = high
        a_lo[2 * m:2 * m + 16, span] = low
    def shifted(start, width):
        return pl.ds(pl.multiple_of(y * H + start, W), width)

    def out_remote(start, width, i):
        return remote(
            obuf.at[:, pl.ds(start, width)], prod.at[:, shifted(start, width)],
            o_send.at[i], o_recv.at[i], {"row": mate},
        )

    def dot(left, right):
        return jnp.dot(left, right, preferred_element_type=jnp.float32)

    def multiply(start, width, i):
        span = pl.ds(start, width)
        high, low = split(bbuf[:, :, span].reshape(R * kb, width))
        acc = dot(a_hi[...], high) + dot(a_hi[...], low) + dot(a_lo[...], high)
        prod[:, shifted(start, width)] = acc[0:m]
        obuf[:, span] = acc[m:2 * m]
        chk[y, :, span] = acc[2 * m:2 * m + 8]
        out_remote(start, width, i).start()

    pairs = NC // 2 - 1
    own.wait()

    @pl.loop(0, pairs)
    def _(i):
        @pl.when(i > 0)
        def _():
            forward(2 * i)

        forward(2 * i + 1)
        multiply(pl.multiple_of(2 * i * W, 2 * W), 2 * W, i)

    for i in range(2):
        forward(2 * pairs + i)
        multiply((2 * pairs + i) * W, W, pairs + i)

    last = same(chk.at[y], c_send, c_recv, {"row": mate})
    last.start()

    total = jnp.zeros((8, m), jnp.float32)
    for i in range(C):
        total += exact_dot(bchk[:, i * kc:(i + 1) * kc], abuf[0, i], ((1,), (1,)))
    cols_out[...] = total[0:2]

    @pl.loop(0, NC)
    def _(j):
        y_copy(j).wait_send()
        for u in range(Z):
            @pl.when((z < Z - 1) & (u < z))
            def _():
                up(u, j).wait_send()

            @pl.when((z > 0) & (u > z))
            def _():
                down(u, j).wait_send()

        for row in (r, mate):
            @pl.when(z < Z - 1)
            def _():
                own_block(row, j, r + 2, up_send).wait_send()

            @pl.when(z > 0)
            def _():
                own_block(row, j, r - 2, dn_send).wait_send()

    for copy in a_sends + small:
        copy.wait_send()
    last.wait()
    rows_out[:, 0:H] = chk[0, 0:2, :]
    rows_out[:, H:2 * H] = chk[1, 0:2, :]

    @pl.loop(0, pairs)
    def _(i):
        out_remote(pl.multiple_of(2 * i * W, 2 * W), 2 * W, i).wait()

    for i in range(2):
        out_remote((2 * pairs + i) * W, W, pairs + i).wait()


def per_device(R, C, a_slab, b_panel, row_weights, col_weights):
    m, kc = a_slab.shape
    kb, n = b_panel.shape
    Z, G, H = R // 2, C // 2, n // 2
    NC = H // WIDTH
    K = R * kb
    f32, bf16 = jnp.float32, jnp.bfloat16
    dma = pltpu.SemaphoreType.DMA
    vmem = pl.BlockSpec(memory_space=pltpu.VMEM)
    scratch = [
        pltpu.VMEM((R, kb, H), f32),
        pltpu.VMEM((m, H), f32),
        pltpu.VMEM((2, C, m, kc), f32),
        pltpu.VMEM((2 * m + 16, K), bf16),
        pltpu.VMEM((2 * m + 16, K), bf16),
        pltpu.VMEM((2, 8, H), f32),
        pltpu.VMEM((8, m), f32),
        pltpu.VMEM((8, n), f32),
        pltpu.VMEM((R, 8, kc), f32),
        pltpu.VMEM((C, 8, kb), f32),
        pltpu.VMEM((C, 8, kc), f32),
        pltpu.VMEM((R, 8, kb), f32),
        pltpu.VMEM((8, K), f32),
        dma,
        dma((NC,)), dma((NC,)),
        dma((R, NC)), dma((R, NC)), dma((Z, NC)),
        dma((3 + 4 * (G - 1),)), dma((2, C)),
        dma((R,)), dma((R,)), dma((C,)), dma((C,)),
        dma((C,)), dma((C,)), dma((R,)), dma((R,)),
        dma((NC // 2 + 1,)), dma((NC // 2 + 1,)),
        dma, dma,
    ]
    return pl.pallas_call(
        functools.partial(kernel, R, C),
        out_shape=(
            pltpu.VMEM((m, n), f32),
            jax.ShapeDtypeStruct((2, n), f32),
            jax.ShapeDtypeStruct((2, m), f32),
        ),
        in_specs=[vmem] * 4,
        out_specs=(vmem, vmem, vmem),
        scratch_shapes=scratch,
        compiler_params=pltpu.CompilerParams(
            collective_id=0, has_side_effects=True, vmem_limit_bytes=46 * 1024 * 1024
        ),
    )(a_slab, b_panel, row_weights, col_weights)


def solution(mesh):
    placed = (P("row", "col"), P("row", "col"), P(None, "row"), P(None, "col"))
    return jax.shard_map(
        functools.partial(per_device, mesh.shape["row"], mesh.shape["col"]),
        mesh=mesh,
        in_specs=placed,
        out_specs=(P("row", "col"), P(None, "col"), P(None, "row")),
        check_vma=False,
    )
```

```python
import functools

import jax
import jax.numpy as jnp
from jax import lax
from jax.experimental import pallas as pl
from jax.experimental.pallas import tpu as pltpu
from jax.sharding import PartitionSpec as P

MESH = pl.DeviceIdType.MESH
WIDTH = 128
AHEAD = 6
PACE = 6
TAIL = 8


def exact_dot(left, right, dims):
    return lax.dot_general(
        left, right, (dims, ((), ())), precision=lax.Precision.HIGHEST, preferred_element_type=jnp.float32
    )


def split(value):
    high = value.astype(jnp.bfloat16)
    return high, (value - high.astype(jnp.float32)).astype(jnp.bfloat16)


def kernel(
    R, C, a_ref, b_ref, rw_ref, cw_ref, prod, rows_out, cols_out,
    bbuf, obuf, abuf, a_hi, a_lo, chk, rwp, cwp, sa, sb, ga, gb, bchk,
    local_sem, y_send, y_recv, up_send, dn_send, z_recv, a_send, a_recv,
    sa_send, sa_recv, sb_send, sb_recv, ga_send, ga_recv, gb_send, gb_recv,
    o_send, o_recv, c_send, c_recv,
):
    Z, G = R // 2, C // 2
    r, c = lax.axis_index("row"), lax.axis_index("col")
    z, y = r // 2, lax.rem(r, 2)
    mate = r + 1 - 2 * y
    sib = c + 1 - 2 * lax.rem(c, 2)
    m, kc = a_ref.shape
    kb, n = b_ref.shape
    H = n // 2
    W = WIDTH
    NC = H // W

    def remote(src, dst, ssem, rsem, where):
        return pltpu.make_async_remote_copy(
            src_ref=src, dst_ref=dst, send_sem=ssem, recv_sem=rsem, device_id=where, device_id_type=MESH
        )

    def same(ref, ssem, rsem, where):
        return remote(ref, ref, ssem, rsem, where)

    barrier = pltpu.get_barrier_semaphore()
    row_peers = [lax.rem(r + d, R) for d in range(1, R)]
    col_peers = [lax.rem(c + d, C) for d in range(1, C)]
    for p in row_peers:
        pl.semaphore_signal(barrier, inc=1, device_id={"row": p}, device_id_type=MESH)
    for p in col_peers:
        pl.semaphore_signal(barrier, inc=1, device_id={"col": p}, device_id_type=MESH)
    own = pltpu.make_async_copy(b_ref.at[:, pl.ds(pl.multiple_of(y * H, H), H)], bbuf.at[r], local_sem)
    own.start()
    abuf[0, c] = a_ref[...]
    pl.semaphore_wait(barrier, R - 1 + C - 1)

    def columns(j):
        return pl.ds(pl.multiple_of(j * W, W), W)

    def y_copy(j):
        src = b_ref.at[:, pl.ds(pl.multiple_of((1 - y) * H + j * W, W), W)]
        return remote(src, bbuf.at[r, :, columns(j)], y_send.at[j], y_recv.at[j], {"row": mate})

    def unit(u, j, to, ssem):
        return same(bbuf.at[pl.ds(2 * u, 2), :, columns(j)], ssem.at[2 * u, j], z_recv.at[u, j], {"row": to})

    def up(u, j):
        return unit(u, j, r + 2, up_send)

    def down(u, j):
        return unit(u, j, r - 2, dn_send)

    same_core = [lax.rem(c + 2 * k, C) for k in range(1, G)]
    a_sends = []

    def a_copy(s, cc, t, where):
        copy = remote(abuf.at[s, cc], abuf.at[t, cc], a_send.at[len(a_sends)], a_recv.at[t, cc], where)
        a_sends.append(copy)
        copy.start()

    def a_wait(t, cc):
        remote(abuf.at[t, cc], abuf.at[t, cc], a_send.at[0], a_recv.at[t, cc], {"row": mate}).wait_recv()

    a_copy(0, c, 1, {"row": mate})
    for p in same_core:
        a_copy(0, c, 0, {"col": p})
    a_copy(0, c, 0, {"col": sib})
    for j in range(2):
        y_copy(j).start()

    def own_block(row, j, to, ssem):
        src = dst = bbuf.at[row, :, columns(j)]
        if row is r:
            src = b_ref.at[:, pl.ds(pl.multiple_of(y * H + j * W, W), W)]
        return remote(src, dst, ssem.at[row, j], z_recv.at[z, j], {"row": to})

    def send_block(row, j):
        @pl.when(z < Z - 1)
        def _():
            own_block(row, j, r + 2, up_send).start()

        @pl.when(z > 0)
        def _():
            own_block(row, j, r - 2, dn_send).start()

    @pl.loop(0, NC)
    def _(j):
        send_block(r, j)

    def send_mate(j):
        y_copy(j).wait_recv()
        send_block(mate, j)

        @pl.when(j + PACE < NC)
        def _():
            y_copy(j + PACE).start()

    def forward(j):
        @pl.when(j + AHEAD < NC)
        def _():
            send_mate(j + AHEAD)

        for d in range(1, Z):
            @pl.when(z - d >= 0)
            def _():
                up(z - d, j).wait_recv()

                @pl.when(z < Z - 1)
                def _():
                    up(z - d, j).start()

            @pl.when(z + d < Z)
            def _():
                down(z + d, j).wait_recv()

                @pl.when(z > 0)
                def _():
                    down(z + d, j).start()

    rwp[...] = jnp.zeros_like(rwp)
    cwp[...] = jnp.zeros_like(cwp)
    rwp[0:2, :] = rw_ref[...]
    cwp[0:2, :] = cw_ref[...]
    sa[r] = exact_dot(rwp[...], a_ref[...], ((1,), (0,)))
    sb[c] = exact_dot(cwp[...], b_ref[...], ((1,), (1,)))

    def spread(buf, slot, peers, axis, ssem, rsem):
        copies = [
            same(buf.at[slot], ssem.at[i], rsem.at[slot], {axis: p}) for i, p in enumerate(peers)
        ]
        for copy in copies:
            copy.start()
        return copies

    def collect(buf, peers, axis, ssem, rsem):
        for p in peers:
            same(buf.at[p], ssem.at[0], rsem.at[p], {axis: p}).wait_recv()

    small = spread(sa, r, row_peers, "row", sa_send, sa_recv)
    small += spread(sb, c, col_peers, "col", sb_send, sb_recv)

    a_wait(1, c)
    for p in same_core:
        a_copy(1, c, 1, {"col": p})
    a_copy(1, c, 1, {"col": sib})
    for j in range(2, PACE):
        y_copy(j).start()
    for j in range(3):
        send_mate(j)

    collect(sa, row_peers, "row", sa_send, sa_recv)
    collect(sb, col_peers, "col", sb_send, sb_recv)
    ga[c] = jnp.sum(sa[...], axis=0)
    gb[r] = jnp.sum(sb[...], axis=0)
    small += spread(ga, c, col_peers, "col", ga_send, ga_recv)
    small += spread(gb, r, row_peers, "row", gb_send, gb_recv)

    for j in range(3, AHEAD):
        send_mate(j)

    for t in range(2):
        for p in same_core:
            a_wait(t, p)
            a_copy(t, p, t, {"col": sib})
    collect(ga, col_peers, "col", ga_send, ga_recv)
    collect(gb, row_peers, "row", gb_send, gb_recv)

    forward(0)

    for t in range(2):
        for k in range(G):
            a_wait(t, lax.rem(sib + 2 * k, C))
    for i in range(R):
        bchk[:, i * kb:(i + 1) * kb] = gb[i]
    for i in range(C):
        span = slice(i * kc, (i + 1) * kc)
        for t in range(2):
            high, low = split(abuf[t, i])
            a_hi[t * m:(t + 1) * m, span] = high
            a_lo[t * m:(t + 1) * m, span] = low
        high, low = split(jnp.concatenate([ga[i], jnp.zeros_like(ga[i])], axis=0))
        a_hi[2 * m:2 * m + 16, span] = high
        a_lo[2 * m:2 * m + 16, span] = low
    def shifted(start, width):
        return pl.ds(pl.multiple_of(y * H + start, W), width)

    def out_remote(start, width, i):
        return remote(
            obuf.at[:, pl.ds(start, width)], prod.at[:, shifted(start, width)],
            o_send.at[i], o_recv.at[i], {"row": mate},
        )

    def dot(left, right):
        return jnp.dot(left, right, preferred_element_type=jnp.float32)

    def multiply(start, width, i):
        span = pl.ds(start, width)
        high, low = split(bbuf[:, :, span].reshape(R * kb, width))
        acc = dot(a_hi[...], high) + dot(a_hi[...], low) + dot(a_lo[...], high)
        prod[:, shifted(start, width)] = acc[0:m]
        obuf[:, span] = acc[m:2 * m]
        chk[y, :, span] = acc[2 * m:2 * m + 8]
        out_remote(start, width, i).start()

    pairs = (NC - TAIL) // 2
    own.wait()

    @pl.loop(0, pairs)
    def _(i):
        @pl.when(i > 0)
        def _():
            forward(2 * i)

        forward(2 * i + 1)
        multiply(pl.multiple_of(2 * i * W, 2 * W), 2 * W, i)

    def rows_copy(start, width, i):
        return same(chk.at[y, :, pl.ds(start, width)], c_send.at[i], c_recv.at[i], {"row": mate})

    bulk = rows_copy(0, 2 * pairs * W, 0)
    bulk.start()
    total = jnp.zeros((8, m), jnp.float32)
    for i in range(C):
        total += exact_dot(bchk[:, i * kc:(i + 1) * kc], abuf[0, i], ((1,), (1,)))
    cols_out[...] = total[0:2]

    @pl.loop(0, TAIL)
    def _(i):
        forward(2 * pairs + i)
        multiply(pl.multiple_of((2 * pairs + i) * W, W), W, pairs + i)

    last = rows_copy(2 * pairs * W, TAIL * W, 1)
    last.start()

    @pl.loop(0, NC)
    def _(j):
        y_copy(j).wait_send()
        for u in range(Z):
            @pl.when((z < Z - 1) & (u < z))
            def _():
                up(u, j).wait_send()

            @pl.when((z > 0) & (u > z))
            def _():
                down(u, j).wait_send()

        for row in (r, mate):
            @pl.when(z < Z - 1)
            def _():
                own_block(row, j, r + 2, up_send).wait_send()

            @pl.when(z > 0)
            def _():
                own_block(row, j, r - 2, dn_send).wait_send()

    for copy in a_sends + small:
        copy.wait_send()
    bulk.wait()
    last.wait()
    rows_out[:, 0:H] = chk[0, 0:2, :]
    rows_out[:, H:2 * H] = chk[1, 0:2, :]

    @pl.loop(0, pairs)
    def _(i):
        out_remote(pl.multiple_of(2 * i * W, 2 * W), 2 * W, i).wait()

    @pl.loop(0, TAIL)
    def _(i):
        out_remote(pl.multiple_of((2 * pairs + i) * W, W), W, pairs + i).wait()


def per_device(R, C, a_slab, b_panel, row_weights, col_weights):
    m, kc = a_slab.shape
    kb, n = b_panel.shape
    Z, G, H = R // 2, C // 2, n // 2
    NC = H // WIDTH
    K = R * kb
    f32, bf16 = jnp.float32, jnp.bfloat16
    dma = pltpu.SemaphoreType.DMA
    vmem = pl.BlockSpec(memory_space=pltpu.VMEM)
    scratch = [
        pltpu.VMEM((R, kb, H), f32),
        pltpu.VMEM((m, H), f32),
        pltpu.VMEM((2, C, m, kc), f32),
        pltpu.VMEM((2 * m + 16, K), bf16),
        pltpu.VMEM((2 * m + 16, K), bf16),
        pltpu.VMEM((2, 8, H), f32),
        pltpu.VMEM((8, m), f32),
        pltpu.VMEM((8, n), f32),
        pltpu.VMEM((R, 8, kc), f32),
        pltpu.VMEM((C, 8, kb), f32),
        pltpu.VMEM((C, 8, kc), f32),
        pltpu.VMEM((R, 8, kb), f32),
        pltpu.VMEM((8, K), f32),
        dma,
        dma((NC,)), dma((NC,)),
        dma((R, NC)), dma((R, NC)), dma((Z, NC)),
        dma((3 + 4 * (G - 1),)), dma((2, C)),
        dma((R,)), dma((R,)), dma((C,)), dma((C,)),
        dma((C,)), dma((C,)), dma((R,)), dma((R,)),
        dma(((NC + TAIL) // 2,)), dma(((NC + TAIL) // 2,)),
        dma((2,)), dma((2,)),
    ]
    return pl.pallas_call(
        functools.partial(kernel, R, C),
        out_shape=(
            pltpu.VMEM((m, n), f32),
            pltpu.VMEM((2, n), f32),
            pltpu.VMEM((2, m), f32),
        ),
        in_specs=[vmem] * 4,
        out_specs=(vmem, vmem, vmem),
        scratch_shapes=scratch,
        compiler_params=pltpu.CompilerParams(
            collective_id=0, has_side_effects=True, vmem_limit_bytes=46 * 1024 * 1024
        ),
    )(a_slab, b_panel, row_weights, col_weights)


def solution(mesh):
    placed = (P("row", "col"), P("row", "col"), P(None, "row"), P(None, "col"))
    return jax.shard_map(
        functools.partial(per_device, mesh.shape["row"], mesh.shape["col"]),
        mesh=mesh,
        in_specs=placed,
        out_specs=(P("row", "col"), P(None, "col"), P(None, "row")),
        check_vma=False,
    )
```
